256 devices in a mesh: head: 16 (over z_hi, x, core), ctx: 16 (over z_lo, y).
Axes of the slice: x: 4, y: 4, z: 8 (z_hi: 2, z_lo: 4; z = z_hi * 4 + z_lo), core: 2. Of those that a mesh axis runs over, the one named last changes fastest.
Arguments:
- queries: bfloat16 [16, 2048, 8192], P('ctx', 'head'), may hold values from -20 to 20
- keys: bfloat16 [16, 2048, 1024], P('ctx', 'head'), may hold values from -20 to 20
- values: bfloat16 [16, 2048, 1024], P('ctx', 'head'), may hold values from -6 to 6
- attended_grad: bfloat16 [16, 2048, 8192], P('ctx', 'head'), may hold values from -6 to 6
- key_blocks: int32 [256, 8], replicated, may hold values from 0 to 255, as said below
- block_counts: int32 [256], replicated, may hold values from 1 to 8
Outputs:
- attended: bfloat16 [16, 2048, 8192], P('ctx', 'head')
- query_grad: bfloat16 [16, 2048, 8192], P('ctx', 'head')
- key_grad: bfloat16 [16, 2048, 1024], P('ctx', 'head')
- value_grad: bfloat16 [16, 2048, 1024], P('ctx', 'head')
The draws below stay inside these ranges and needn't reach their ends.
Inputs may be any that keep to these rules, and one draw needn't show every extreme that they name: `key_blocks`: row b lists 8 different key blocks, the first of them b itself.
All inputs are finite; a program needn't handle non-finite values.
Results may differ from the reference program's by a relative error of at most 0.029.
Values may be sent and summed in bfloat16 or wider, within the bound.
No kernel may reach another device: no remote copies, remote signals or barrier semaphores. Data moves between devices by JAX's collectives and lax.ppermute only.
A program may use at most 192 MiB of HBM per device.

```python
import jax
import jax.numpy as jnp
from jax import lax

HQ = 64
KVH = 8
HD = 128
BLK = 128
MAXK = 8
PIECES = 16
SEQ_DEV = 2048
NB = 256


def draw_queries(key, part):
    key = jax.random.fold_in(key, 1)
    count = PIECES * SEQ_DEV
    result = jnp.clip(jax.random.normal(key, (count, KVH, HQ // KVH, HD), jnp.float32), -4.0, 4.0)
    return result.reshape(PIECES, SEQ_DEV, HQ * HD).astype(jnp.bfloat16)


def draw_keys(key, part):
    key = jax.random.fold_in(key, 2)
    count = PIECES * SEQ_DEV
    result = jnp.clip(jax.random.normal(key, (count, KVH, HD), jnp.float32), -4.0, 4.0)
    return result.reshape(PIECES, SEQ_DEV, KVH * HD).astype(jnp.bfloat16)


def pick_offsets(row_key):
    return jax.random.permutation(row_key, NB - 1)[:MAXK - 1]


def draw_key_blocks(key, part):
    key = jax.random.fold_in(key, 3)
    row_keys = jax.random.split(key, NB)
    offsets = jax.vmap(pick_offsets)(row_keys).astype(jnp.int32)
    own_block = jnp.arange(NB, dtype=jnp.int32)
    far_blocks = (own_block[:, None] + 1 + offsets) % NB
    return jnp.concatenate([own_block[:, None], far_blocks], axis=1).astype(jnp.int32)


def draw_block_counts(key, part):
    key = jax.random.fold_in(key, 4)
    block_index = jnp.arange(NB, dtype=jnp.int32)
    ceiling = 1 + (MAXK - 1) * block_index * block_index // ((NB - 1) * (NB - 1))
    result = 1 + jax.random.randint(key, (NB,), 0, ceiling)
    return jnp.where(block_index == NB - 1, MAXK, result).astype(jnp.int32)


def shard_levels(rng, dims, pieces, least, top_value):
    def one(dim, blocks):
        steps = jax.random.uniform(jax.random.fold_in(jax.random.fold_in(rng, 6), dim), (blocks,), jnp.float32, least / len(pieces), top_value / len(pieces))
        return jnp.repeat(jnp.exp(steps), dims[dim] // blocks).reshape((-1,) + (1,) * (len(dims) - dim - 1))

    factor_of = one(*pieces[0])
    for cut in pieces[1:]:
        factor_of = factor_of * one(*cut)
    return factor_of


def scatter_about(key, dims, spread, bound, cuts=(), kind=jnp.bfloat16):
    values = jax.random.normal(key, dims, jnp.float32) * spread
    if len(cuts) > 0:
        values = shard_levels(key, dims, cuts, -0.22, 0.18) * values
    return jnp.clip(values, min=-bound, max=bound).astype(kind)


def setup_inputs(seed: int = 0) -> dict:
    splits = jax.random.split(jax.random.key(seed), 7)
    queries = draw_queries(jax.random.fold_in(splits[6], 71), 0)
    keys = draw_keys(jax.random.fold_in(splits[6], 71), 0)
    values = scatter_about(splits[2], (PIECES, SEQ_DEV, KVH * HD), 1.0, 6.0, ((0, 16), (1, 16)))
    attended_grad = scatter_about(splits[3], (PIECES, SEQ_DEV, HQ * HD), 1.0, 6.0, ((0, 16), (1, 16)))
    key_blocks = draw_key_blocks(jax.random.fold_in(splits[6], 71), 0)
    block_counts = draw_block_counts(jax.random.fold_in(splits[6], 71), 0)
    return {"queries": queries, "keys": keys, "values": values, "attended_grad": attended_grad, "key_blocks": key_blocks, "block_counts": block_counts}


low_value = -1.0e30


def rounded(array):
    return lax.optimization_barrier(array.astype(jnp.bfloat16)).astype(jnp.float32)


def reference(queries, keys, values, attended_grad, key_blocks, block_counts):
    all_blocks = key_blocks.shape[0]
    group_size = HQ // KVH
    inv_root = HD ** -0.5
    highest = lax.Precision.HIGHEST
    query_all = queries.reshape(all_blocks, BLK, KVH, group_size, HD)
    grad_all = attended_grad.reshape(all_blocks, BLK, KVH, group_size, HD)
    key_all = keys.reshape(all_blocks, BLK, KVH, HD)
    value_all = values.reshape(all_blocks, BLK, KVH, HD)

    def one_block(running, block_index):
        key_sum, value_sum = running
        query_part = query_all[block_index].astype(jnp.float32)
        grad_part = grad_all[block_index].astype(jnp.float32)
        chosen = key_blocks[block_index].astype(jnp.int32)
        live = jnp.arange(MAXK, dtype=jnp.int32) < block_counts[block_index]
        seen = jnp.repeat(live, BLK)
        key_part = key_all[chosen].reshape(MAXK * BLK, KVH, HD).astype(jnp.float32)
        value_part = value_all[chosen].reshape(MAXK * BLK, KVH, HD).astype(jnp.float32)
        scores = jnp.einsum("qkgd,skd->kgqs", query_part, key_part, precision=highest) * inv_root
        scores = jnp.where(seen, scores, low_value)
        row_top = jnp.max(scores, axis=-1, keepdims=True)
        expon = jnp.where(seen, jnp.exp(scores - row_top), 0.0)
        probs = expon / jnp.sum(expon, axis=-1, keepdims=True)
        probs_low = rounded(probs)
        attended = jnp.einsum("kgqs,skd->qkgd", probs_low, value_part, precision=highest).astype(jnp.bfloat16)
        row_delta = jnp.sum(grad_part * attended.astype(jnp.float32), axis=-1)
        row_delta = jnp.transpose(row_delta, (1, 2, 0))
        dprobs = jnp.einsum("qkgd,skd->kgqs", grad_part, value_part, precision=highest)
        dscores = rounded(probs * (dprobs - row_delta[..., None]) * inv_root)
        query_grad = jnp.einsum("kgqs,skd->qkgd", dscores, key_part, precision=highest).astype(jnp.bfloat16)
        key_add = jnp.einsum("kgqs,qkgd->skd", dscores, query_part, precision=highest)
        value_add = jnp.einsum("kgqs,qkgd->skd", probs_low, grad_part, precision=highest)
        key_sum = key_sum.at[chosen].add(key_add.reshape(MAXK, BLK, KVH * HD))
        value_sum = value_sum.at[chosen].add(value_add.reshape(MAXK, BLK, KVH * HD))
        return (key_sum, value_sum), (attended, query_grad)

    start = (jnp.zeros((all_blocks, BLK, KVH * HD), jnp.float32), jnp.zeros((all_blocks, BLK, KVH * HD), jnp.float32))
    sums, outputs = lax.scan(one_block, start, jnp.arange(all_blocks, dtype=jnp.int32))
    key_sum, value_sum = sums
    attended, query_grad = outputs
    return (attended.reshape(PIECES, SEQ_DEV, HQ * HD),
            query_grad.reshape(PIECES, SEQ_DEV, HQ * HD),
            key_sum.astype(jnp.bfloat16).reshape(PIECES, SEQ_DEV, KVH * HD),
            value_sum.astype(jnp.bfloat16).reshape(PIECES, SEQ_DEV, KVH * HD))
```

```python
import functools

import jax
import jax.numpy as jnp
from jax import lax
from jax.experimental import pallas as pl
from jax.experimental.pallas import tpu as pltpu
from jax.sharding import Mesh, PartitionSpec as P

HQ = 64
KVH = 8
HD = 128
BLK = 128
MAXK = 8
NB = 256

AXES = ("zh", "x", "k", "zl", "y")
SIZES = (2, 4, 2, 4, 4)
ROWS = (("zl", "y"), ("zh", "x", "k"), None)
POOL = ("k", "y")
PLANE = ("zl", "zh", "x")
EVERY = ("zl", "y", "zh", "x", "k")

MEMBERS = 8
POOLS = 32
MOST_FAR = MEMBERS * (MAXK - 1)
PAIR_ROOM = POOLS * MOST_FAR
STRIDE = 64
CLASSES = (16, 20, 24, 28, 32, 36, 40, 48, MOST_FAR)
UNROLL = 8
WIDE = (HQ // KVH) * HD
SLAB = 2 * WIDE + 2 * HD
LANES = 256
INV_ROOT = HD**-0.5

any_spec = pl.BlockSpec(memory_space=pl.ANY)
smem_spec = pl.BlockSpec(memory_space=pltpu.SMEM)
vmem_spec = pl.BlockSpec(memory_space=pltpu.VMEM)
roomy = pltpu.CompilerParams(vmem_limit_bytes=52 * 1024 * 1024)


def member_block(zl, zh, x, member):
    k, y = member // 4, member % 4
    return (zl * 4 + y) * 16 + zh * 8 + x * 2 + k


def plan_kernel(blocks, counts, src, dst, meta):
    def one_pool(d, carry):
        t, most = carry
        zl, zh, x = d // 8, (d // 4) % 2, d % 4

        def one_member(m, inner):
            t, r = inner
            b = member_block(zl, zh, x, m)
            extra = counts[b] - 1

            def one_slot(j, _):
                src[t + j] = blocks[b * MAXK + 1 + j]
                dst[t + j] = d * STRIDE + r + j
                return 0

            lax.fori_loop(0, extra, one_slot, 0)
            return (t + extra, r + extra)

        t, r = lax.fori_loop(0, MEMBERS, one_member, (t, jnp.int32(0)))
        return (t, jnp.maximum(most, r))

    total, most = lax.fori_loop(0, POOLS, one_pool, (jnp.int32(0), jnp.int32(0)))
    meta[0] = total
    meta[1] = most


def make_plan(blocks, counts):
    shape = jax.ShapeDtypeStruct((PAIR_ROOM,), jnp.int32)
    return pl.pallas_call(
        plan_kernel,
        out_shape=(shape, shape, jax.ShapeDtypeStruct((2,), jnp.int32)),
        in_specs=[smem_spec] * 2,
        out_specs=(smem_spec,) * 3,
        name="plan",
    )(blocks, counts)


def pack_kernel(place, q, g, k, v, *rest):
    slabs, sems = rest[:MEMBERS], rest[MEMBERS]
    me = place[0]
    copies = []
    for s in range(MEMBERS):
        to = me ^ s
        wide = pl.ds(pl.multiple_of(to * WIDE, WIDE), WIDE)
        slim = pl.ds(pl.multiple_of(to * HD, HD), HD)
        parts = (
            (q.at[:, wide], slabs[s].at[:, 0:WIDE]),
            (g.at[:, wide], slabs[s].at[:, WIDE : 2 * WIDE]),
            (k.at[:, slim], slabs[s].at[:, 2 * WIDE : 2 * WIDE + HD]),
            (v.at[:, slim], slabs[s].at[:, 2 * WIDE + HD : SLAB]),
        )
        for i, (a, b) in enumerate(parts):
            copies.append(pltpu.make_async_copy(a, b, sems.at[s * 4 + i]))
    for copy in copies:
        copy.start()
    for copy in copies:
        copy.wait()


def pack(place, q, g, k, v):
    shape = jax.ShapeDtypeStruct((BLK, SLAB), jnp.bfloat16)
    return pl.pallas_call(
        pack_kernel,
        out_shape=(shape,) * MEMBERS,
        in_specs=[smem_spec] + [any_spec] * 4,
        out_specs=(vmem_spec,) * MEMBERS,
        scratch_shapes=[pltpu.SemaphoreType.DMA((4 * MEMBERS,))],
        compiler_params=roomy,
        name="pack",
    )(place, q, g, k, v)


def unpack_kernel(place, *rest):
    slabs = rest[:MEMBERS]
    out, dq, dk, dv, sems = rest[MEMBERS:]
    me = place[0]
    copies = []
    for s in range(MEMBERS):
        to = me ^ s
        wide = pl.ds(pl.multiple_of(to * WIDE, WIDE), WIDE)
        slim = pl.ds(pl.multiple_of(to * HD, HD), HD)
        parts = (
            (slabs[s].at[:, 0:WIDE], out.at[:, wide]),
            (slabs[s].at[:, WIDE : 2 * WIDE], dq.at[:, wide]),
            (slabs[s].at[:, 2 * WIDE : 2 * WIDE + HD], dk.at[:, slim]),
            (slabs[s].at[:, 2 * WIDE + HD : SLAB], dv.at[:, slim]),
        )
        for i, (a, b) in enumerate(parts):
            copies.append(pltpu.make_async_copy(a, b, sems.at[s * 4 + i]))
    for copy in copies:
        copy.start()
    for copy in copies:
        copy.wait()


def unpack(place, slabs):
    wide = jax.ShapeDtypeStruct((BLK, HQ * HD), jnp.bfloat16)
    slim = jax.ShapeDtypeStruct((BLK, KVH * HD), jnp.bfloat16)
    return pl.pallas_call(
        unpack_kernel,
        out_shape=(wide, wide, slim, slim),
        in_specs=[smem_spec] + [vmem_spec] * MEMBERS,
        out_specs=(any_spec,) * 4,
        scratch_shapes=[pltpu.SemaphoreType.DMA((4 * MEMBERS,))],
        compiler_params=roomy,
        name="unpack",
    )(place, *slabs)


def each_pair(count, one):
    def several(i, _):
        for u in range(UNROLL):
            one(i * UNROLL + u)
        return 0

    def single(t, _):
        one(t)
        return 0

    lax.fori_loop(0, count // UNROLL, several, 0)
    lax.fori_loop((count // UNROLL) * UNROLL, count, single, 0)


def gather_kernel(room, src, dst, meta, pieces, out):
    def one(t):
        at = dst[t]
        out[(at // STRIDE) * room + at % STRIDE] = pieces[src[t]]

    each_pair(meta[0], one)


def gather_pieces(room, src, dst, meta, pieces):
    return pl.pallas_call(
        functools.partial(gather_kernel, room),
        out_shape=jax.ShapeDtypeStruct((POOLS * room, 8, HD), jnp.bfloat16),
        in_specs=[smem_spec] * 3 + [vmem_spec],
        out_specs=vmem_spec,
        compiler_params=roomy,
        name="gather_pieces",
    )(src, dst, meta, pieces)


def add_kernel(room, src, dst, meta, terms, out, total):
    total[...] = jnp.zeros_like(total)

    def one(t):
        at = dst[t]
        to = src[t]
        total[to] += terms[(at // STRIDE) * room + at % STRIDE].astype(jnp.float32)

    each_pair(meta[0], one)
    out[...] = total[...].astype(jnp.bfloat16)


def add_pieces(room, src, dst, meta, terms):
    return pl.pallas_call(
        functools.partial(add_kernel, room),
        out_shape=jax.ShapeDtypeStruct((NB, 8, HD), jnp.bfloat16),
        in_specs=[smem_spec] * 3 + [vmem_spec],
        out_specs=vmem_spec,
        scratch_shapes=[pltpu.VMEM((NB, 8, HD), jnp.float32)],
        compiler_params=roomy,
        name="add_pieces",
    )(src, dst, meta, terms)


def nt(a, b):
    return lax.dot_general(a, b, (((1,), (1,)), ((), ())), preferred_element_type=jnp.float32)


def nn(a, b):
    return jnp.dot(a, b, preferred_element_type=jnp.float32)


def fold(a, how):
    return how(a.reshape(BLK // 8, 8, a.shape[1]), axis=0)


def attend_kernel(place, counts, far_away, *rest):
    slabs = rest[:MEMBERS]
    outs = rest[MEMBERS : 2 * MEMBERS]
    far_made = rest[2 * MEMBERS]
    held, made, far, far_grad, rows_q, rows_g, kv, kv_t, expo, dpro, out_t, dq_t = rest[
        2 * MEMBERS + 1 : 2 * MEMBERS + 13
    ]
    first, sems_in, sems_out, sems_far, sems_made = rest[2 * MEMBERS + 13 :]
    me, zl, zh, x = place[0], place[1], place[2], place[3]
    for s in range(MEMBERS):
        pltpu.make_async_copy(slabs[s], held.at[s], sems_in.at[s]).start()
    base = jnp.int32(0)
    for m in range(MEMBERS):
        first[m] = base
        base = base + counts[member_block(zl, zh, x, m)] - 1
    used = base

    def far_in(r):
        return pltpu.make_async_copy(far_away.at[r], far.at[r], sems_far.at[r])

    def far_out(r):
        return pltpu.make_async_copy(far_grad.at[r], far_made.at[r], sems_made.at[r])

    def fetch(r, _):
        far_in(r).start()
        return 0

    lax.fori_loop(0, used, fetch, 0)

    def one_block(s, _):
        pltpu.make_async_copy(slabs[0], held.at[s], sems_in.at[s]).wait()
        m = me ^ s
        live = counts[member_block(zl, zh, x, m)]
        start = first[m]
        for h in range(HQ // KVH):
            rows_q[h * BLK : (h + 1) * BLK, :] = held[s, :, h * HD : (h + 1) * HD]
            rows_g[h * BLK : (h + 1) * BLK, :] = held[s, :, WIDE + h * HD : WIDE + (h + 1) * HD]

        def place_pair(j, k_part, v_part):
            kv[j, 0:BLK, :] = k_part
            kv[j, BLK : 2 * BLK, :] = v_part
            kv_t[j, 0:BLK, :] = k_part.T
            kv_t[j, BLK : 2 * BLK, :] = v_part.T

        place_pair(0, held[s, :, 2 * WIDE : 2 * WIDE + HD], held[s, :, 2 * WIDE + HD : SLAB])

        def place_far(j, _):
            far_in(start + j - 1).wait()
            place_pair(j, far[start + j - 1, 0:BLK, :], far[start + j - 1, BLK : 2 * BLK, :])
            return 0

        lax.fori_loop(1, live, place_far, 0)

        def scores(j, tops):
            k_part = kv[j, 0:BLK, :]
            new = []
            for c in range(WIDE // LANES):
                cols = slice(c * LANES, (c + 1) * LANES)
                part = nt(k_part, rows_q[cols, :])
                expo[j, :, cols] = part
                new.append(jnp.maximum(tops[c], fold(part, jnp.max)))
            return tuple(new)

        low = jnp.full((8, LANES), -1e30, jnp.float32)
        tops = lax.fori_loop(0, live, scores, (low,) * (WIDE // LANES))
        tops = [jnp.max(a, axis=0, keepdims=True) for a in tops]

        def exps(j, sums):
            v_part = kv[j, BLK : 2 * BLK, :]
            new = []
            for c in range(WIDE // LANES):
                cols = slice(c * LANES, (c + 1) * LANES)
                e = jnp.exp((expo[j, :, cols] - tops[c]) * INV_ROOT)
                d = nt(v_part, rows_g[cols, :])
                expo[j, :, cols] = e
                dpro[j, :, cols] = d
                total, delta = sums[c]
                new.append((total + fold(e, jnp.sum), delta + fold(e * d, jnp.sum)))
            return tuple(new)

        nil = jnp.zeros((8, LANES), jnp.float32)
        sums = lax.fori_loop(0, live, exps, ((nil, nil),) * (WIDE // LANES))
        inverse, delta = [], []
        for total, weighted in sums:
            one_over = 1.0 / jnp.sum(total, axis=0, keepdims=True)
            inverse.append(one_over)
            delta.append(jnp.sum(weighted, axis=0, keepdims=True) * one_over)
        out_t[...] = jnp.zeros_like(out_t)
        dq_t[...] = jnp.zeros_like(dq_t)

        def grads(j, _):
            k_t = kv_t[j, 0:BLK, :]
            v_t = kv_t[j, BLK : 2 * BLK, :]
            dk = jnp.zeros((BLK, HD), jnp.float32)
            dv = jnp.zeros((BLK, HD), jnp.float32)
            for c in range(WIDE // LANES):
                cols = slice(c * LANES, (c + 1) * LANES)
                p = expo[j, :, cols] * inverse[c]
                ds = (p * (dpro[j, :, cols] - delta[c]) * INV_ROOT).astype(jnp.bfloat16)
                p = p.astype(jnp.bfloat16)
                out_t[:, cols] += nn(v_t, p)
                dq_t[:, cols] += nn(k_t, ds)
                dv += nn(p, rows_g[cols, :])
                dk += nn(ds, rows_q[cols, :])
            dk = dk.astype(jnp.bfloat16)
            dv = dv.astype(jnp.bfloat16)

            @pl.when(j == 0)
            def _():
                made[s, :, 2 * WIDE : 2 * WIDE + HD] = dk
                made[s, :, 2 * WIDE + HD : SLAB] = dv

            @pl.when(j > 0)
            def _():
                far_grad[start + j - 1, 0:BLK, :] = dk
                far_grad[start + j - 1, BLK : 2 * BLK, :] = dv
                far_out(start + j - 1).start()

            return 0

        lax.fori_loop(0, live, grads, 0)
        for h in range(HQ // KVH):
            cols = slice(h * HD, (h + 1) * HD)
            made[s, :, cols] = out_t[:, cols].T.astype(jnp.bfloat16)
            made[s, :, WIDE + h * HD : WIDE + (h + 1) * HD] = dq_t[:, cols].T.astype(jnp.bfloat16)
        for i in range(MEMBERS):

            @pl.when(s == i)
            def _():
                pltpu.make_async_copy(made.at[i], outs[i], sems_out.at[i]).start()

        return 0

    lax.fori_loop(0, MEMBERS, one_block, 0)
    for i in range(MEMBERS):
        pltpu.make_async_copy(made.at[i], outs[i], sems_out.at[i]).wait()

    def finish(r, _):
        far_out(r).wait()
        return 0

    lax.fori_loop(0, used, finish, 0)


def attend(place, counts, far, slabs):
    slab = jax.ShapeDtypeStruct((BLK, SLAB), jnp.bfloat16)
    result = pl.pallas_call(
        attend_kernel,
        out_shape=(slab,) * MEMBERS
        + (jax.ShapeDtypeStruct((MOST_FAR, 2 * BLK, HD), jnp.bfloat16),),
        in_specs=[smem_spec] * 2 + [any_spec] * (MEMBERS + 1),
        out_specs=(any_spec,) * (MEMBERS + 1),
        scratch_shapes=[
            pltpu.VMEM((MEMBERS, BLK, SLAB), jnp.bfloat16),
            pltpu.VMEM((MEMBERS, BLK, SLAB), jnp.bfloat16),
            pltpu.VMEM((MOST_FAR, 2 * BLK, HD), jnp.bfloat16),
            pltpu.VMEM((MOST_FAR, 2 * BLK, HD), jnp.bfloat16),
            pltpu.VMEM((WIDE, HD), jnp.bfloat16),
            pltpu.VMEM((WIDE, HD), jnp.bfloat16),
            pltpu.VMEM((MAXK, 2 * BLK, HD), jnp.bfloat16),
            pltpu.VMEM((MAXK, 2 * BLK, HD), jnp.bfloat16),
            pltpu.VMEM((MAXK, BLK, WIDE), jnp.float32),
            pltpu.VMEM((MAXK, BLK, WIDE), jnp.float32),
            pltpu.VMEM((HD, WIDE), jnp.float32),
            pltpu.VMEM((HD, WIDE), jnp.float32),
            pltpu.SMEM((MEMBERS,), jnp.int32),
            pltpu.SemaphoreType.DMA((MEMBERS,)),
            pltpu.SemaphoreType.DMA((MEMBERS,)),
            pltpu.SemaphoreType.DMA((MOST_FAR,)),
            pltpu.SemaphoreType.DMA((MOST_FAR,)),
        ],
        compiler_params=roomy,
        name="attend",
    )(place, counts, far, *slabs)
    return result[:MEMBERS], result[MEMBERS]


def trade(array, axes):
    return lax.all_to_all(array, axes, split_axis=0, concat_axis=0, tiled=True)


def swap(slabs):
    return (slabs[0],) + tuple(
        lax.ppermute(slabs[s], POOL, [(i, i ^ s) for i in range(MEMBERS)])
        for s in range(1, MEMBERS)
    )


def pick(meta, branches):
    which = sum((meta[1] > room).astype(jnp.int32) for room in CLASSES[:-1])
    return lax.switch(which, branches)


def body(queries, keys, values, attended_grad, key_blocks, block_counts):
    zl, zh, x = (lax.axis_index(a) for a in PLANE)
    place = jnp.stack([lax.axis_index("k") * 4 + lax.axis_index("y"), zl, zh, x])
    place = place.astype(jnp.int32)
    q, k, v, g = (a[0] for a in (queries, keys, values, attended_grad))
    src, dst, meta = make_plan(key_blocks.reshape(-1), block_counts)

    both = jnp.concatenate([k, v], axis=0)
    spread = both.reshape(4, 2, 4, 8, 2, 4, HD).transpose(0, 5, 1, 2, 4, 3, 6)
    pieces = trade(spread.reshape(NB, 8, HD), EVERY)
    slabs = swap(pack(place, q, g, k, v))

    def bring(room):
        def run():
            sent = gather_pieces(room, src, dst, meta, pieces)
            came = trade(sent.reshape(POOLS, room, 8, HD), PLANE)
            far = came.transpose(1, 0, 2, 3).reshape(room, 2 * BLK, HD)
            return jnp.pad(far, ((0, MOST_FAR - room), (0, 0), (0, 0)))

        return run

    far = pick(meta, [bring(room) for room in CLASSES])
    made, far_grad = attend(place, block_counts, far, slabs)

    def give(room):
        def run():
            terms = far_grad[:room].reshape(room, POOLS, 8, HD).transpose(1, 0, 2, 3)
            came = trade(terms, PLANE)
            return add_pieces(room, src, dst, meta, came.reshape(POOLS * room, 8, HD))

        return run

    sums = pick(meta, [give(room) for room in CLASSES])
    home = trade(sums, EVERY).reshape(4, 4, 2, 4, 2, 8, HD).transpose(0, 2, 3, 5, 4, 1, 6)
    home = home.reshape(2, BLK, KVH * HD).astype(jnp.float32)
    attended, query_grad, dk, dv = unpack(place, swap(made))
    key_grad = (dk.astype(jnp.float32) + home[0]).astype(jnp.bfloat16)
    value_grad = (dv.astype(jnp.float32) + home[1]).astype(jnp.bfloat16)
    return attended[None], query_grad[None], key_grad[None], value_grad[None]


def solution(mesh):
    fine = Mesh(mesh.devices.reshape(SIZES), AXES)
    rows = P(*ROWS)
    return jax.shard_map(
        body,
        mesh=fine,
        in_specs=(rows,) * 4 + (P(), P()),
        out_specs=(rows,) * 4,
        check_vma=False,
    )
```

```python
import functools

import jax
import jax.numpy as jnp
from jax import lax
from jax.experimental import pallas as pl
from jax.experimental.pallas import tpu as pltpu
from jax.sharding import Mesh, PartitionSpec as P

HQ = 64
KVH = 8
HD = 128
BLK = 128
MAXK = 8
NB = 256

AXES = ("zh", "x", "k", "zl", "y")
SIZES = (2, 4, 2, 4, 4)
ROWS = (("zl", "y"), ("zh", "x", "k"), None)
POOL = ("k", "y")
PLANE = ("zl", "zh", "x")
EVERY = ("zl", "y", "zh", "x", "k")

MEMBERS = 8
POOLS = 32
MOST_FAR = MEMBERS * (MAXK - 1)
PAIR_ROOM = POOLS * MOST_FAR
STRIDE = 64
CLASSES = (16, 20, 24, 28, 32, 36, 40, 48, MOST_FAR)
UNROLL = 8
WIDE = (HQ // KVH) * HD
SLAB = 2 * WIDE + 2 * HD
LANES = 256
INV_ROOT = HD**-0.5

any_spec = pl.BlockSpec(memory_space=pl.ANY)
smem_spec = pl.BlockSpec(memory_space=pltpu.SMEM)
vmem_spec = pl.BlockSpec(memory_space=pltpu.VMEM)
roomy = pltpu.CompilerParams(vmem_limit_bytes=52 * 1024 * 1024)


def member_block(zl, zh, x, member):
    k, y = member // 4, member % 4
    return (zl * 4 + y) * 16 + zh * 8 + x * 2 + k


def plan_kernel(blocks, counts, src, dst, meta):
    def one_pool(d, carry):
        t, most = carry
        zl, zh, x = d // 8, (d // 4) % 2, d % 4

        def one_member(m, inner):
            t, r = inner
            b = member_block(zl, zh, x, m)
            extra = counts[b] - 1

            for j in range(MAXK - 1):
                src[t + j] = blocks[b * MAXK + 1 + j]
                dst[t + j] = d * STRIDE + r + j
            return (t + extra, r + extra)

        inner = (t, jnp.int32(0))
        for m in range(MEMBERS):
            inner = one_member(m, inner)
        t, r = inner
        return (t, jnp.maximum(most, r))

    total, most = lax.fori_loop(0, POOLS, one_pool, (jnp.int32(0), jnp.int32(0)))
    meta[0] = total
    meta[1] = most


def make_plan(blocks, counts):
    shape = jax.ShapeDtypeStruct((PAIR_ROOM + MAXK,), jnp.int32)
    return pl.pallas_call(
        plan_kernel,
        out_shape=(shape, shape, jax.ShapeDtypeStruct((2,), jnp.int32)),
        in_specs=[smem_spec] * 2,
        out_specs=(smem_spec,) * 3,
        name="plan",
    )(blocks, counts)


def pack_kernel(place, q, g, k, v, *rest):
    slabs, sems = rest[:MEMBERS], rest[MEMBERS]
    me = place[0]
    copies = []
    for s in range(MEMBERS):
        to = me ^ s
        wide = pl.ds(pl.multiple_of(to * WIDE, WIDE), WIDE)
        slim = pl.ds(pl.multiple_of(to * HD, HD), HD)
        parts = (
            (q.at[:, wide], slabs[s].at[:, 0:WIDE]),
            (g.at[:, wide], slabs[s].at[:, WIDE : 2 * WIDE]),
            (k.at[:, slim], slabs[s].at[:, 2 * WIDE : 2 * WIDE + HD]),
            (v.at[:, slim], slabs[s].at[:, 2 * WIDE + HD : SLAB]),
        )
        for i, (a, b) in enumerate(parts):
            copies.append(pltpu.make_async_copy(a, b, sems.at[s * 4 + i]))
    for copy in copies:
        copy.start()
    for copy in copies:
        copy.wait()


def pack(place, q, g, k, v):
    shape = jax.ShapeDtypeStruct((BLK, SLAB), jnp.bfloat16)
    return pl.pallas_call(
        pack_kernel,
        out_shape=(shape,) * MEMBERS,
        in_specs=[smem_spec] + [any_spec] * 4,
        out_specs=(vmem_spec,) * MEMBERS,
        scratch_shapes=[pltpu.SemaphoreType.DMA((4 * MEMBERS,))],
        compiler_params=roomy,
        name="pack",
    )(place, q, g, k, v)


def unpack_kernel(place, *rest):
    slabs = rest[:MEMBERS]
    out, dq, dk, dv, sems = rest[MEMBERS:]
    me = place[0]
    copies = []
    for s in range(MEMBERS):
        to = me ^ s
        wide = pl.ds(pl.multiple_of(to * WIDE, WIDE), WIDE)
        slim = pl.ds(pl.multiple_of(to * HD, HD), HD)
        parts = (
            (slabs[s].at[:, 0:WIDE], out.at[:, wide]),
            (slabs[s].at[:, WIDE : 2 * WIDE], dq.at[:, wide]),
            (slabs[s].at[:, 2 * WIDE : 2 * WIDE + HD], dk.at[:, slim]),
            (slabs[s].at[:, 2 * WIDE + HD : SLAB], dv.at[:, slim]),
        )
        for i, (a, b) in enumerate(parts):
            copies.append(pltpu.make_async_copy(a, b, sems.at[s * 4 + i]))
    for copy in copies:
        copy.start()
    for copy in copies:
        copy.wait()


def unpack(place, slabs):
    wide = jax.ShapeDtypeStruct((BLK, HQ * HD), jnp.bfloat16)
    slim = jax.ShapeDtypeStruct((BLK, KVH * HD), jnp.bfloat16)
    return pl.pallas_call(
        unpack_kernel,
        out_shape=(wide, wide, slim, slim),
        in_specs=[smem_spec] + [vmem_spec] * MEMBERS,
        out_specs=(any_spec,) * 4,
        scratch_shapes=[pltpu.SemaphoreType.DMA((4 * MEMBERS,))],
        compiler_params=roomy,
        name="unpack",
    )(place, *slabs)


def each_pair(count, one):
    def several(i, _):
        for u in range(UNROLL):
            one(i * UNROLL + u)
        return 0

    def single(t, _):
        one(t)
        return 0

    lax.fori_loop(0, count // UNROLL, several, 0)
    lax.fori_loop((count // UNROLL) * UNROLL, count, single, 0)


def gather_kernel(room, src, dst, meta, pieces, out):
    def one(t):
        at = dst[t]
        out[(at // STRIDE) * room + at % STRIDE] = pieces[src[t]]

    each_pair(meta[0], one)


def gather_pieces(room, src, dst, meta, pieces):
    return pl.pallas_call(
        functools.partial(gather_kernel, room),
        out_shape=jax.ShapeDtypeStruct((POOLS * room, 8, HD), jnp.bfloat16),
        in_specs=[smem_spec] * 3 + [vmem_spec],
        out_specs=vmem_spec,
        compiler_params=roomy,
        name="gather_pieces",
    )(src, dst, meta, pieces)


def add_kernel(room, src, dst, meta, terms, out, total):
    total[...] = jnp.zeros_like(total)

    def one(t):
        at = dst[t]
        to = src[t]
        total[to] += terms[(at // STRIDE) * room + at % STRIDE].astype(jnp.float32)

    each_pair(meta[0], one)
    out[...] = total[...].astype(jnp.bfloat16)


def add_pieces(room, src, dst, meta, terms):
    return pl.pallas_call(
        functools.partial(add_kernel, room),
        out_shape=jax.ShapeDtypeStruct((NB, 8, HD), jnp.bfloat16),
        in_specs=[smem_spec] * 3 + [vmem_spec],
        out_specs=vmem_spec,
        scratch_shapes=[pltpu.VMEM((NB, 8, HD), jnp.float32)],
        compiler_params=roomy,
        name="add_pieces",
    )(src, dst, meta, terms)


def nt(a, b):
    return lax.dot_general(a, b, (((1,), (1,)), ((), ())), preferred_element_type=jnp.float32)


def nn(a, b):
    return jnp.dot(a, b, preferred_element_type=jnp.float32)


def fold(a, how):
    return how(a.reshape(BLK // 8, 8, a.shape[1]), axis=0)


def attend_kernel(place, counts, far_away, *rest):
    slabs = rest[:MEMBERS]
    outs = rest[MEMBERS : 2 * MEMBERS]
    far_made = rest[2 * MEMBERS]
    held, made, far, far_grad, rows_q, rows_g, kv, kv_t, expo, dpro, out_t, dq_t = rest[
        2 * MEMBERS + 1 : 2 * MEMBERS + 13
    ]
    first, sems_in, sems_out, sems_far, sems_made = rest[2 * MEMBERS + 13 :]
    me, zl, zh, x = place[0], place[1], place[2], place[3]
    for s in range(MEMBERS):
        pltpu.make_async_copy(slabs[s], held.at[s], sems_in.at[s]).start()
    base = jnp.int32(0)
    for m in range(MEMBERS):
        first[m] = base
        base = base + counts[member_block(zl, zh, x, m)] - 1
    used = base

    def far_in(r):
        return pltpu.make_async_copy(far_away.at[r], far.at[r], sems_far.at[r])

    def far_out(r):
        return pltpu.make_async_copy(far_grad.at[r], far_made.at[r], sems_made.at[r])

    def fetch(r, _):
        far_in(r).start()
        return 0

    lax.fori_loop(0, used, fetch, 0)

    def one_block(s, _):
        pltpu.make_async_copy(slabs[0], held.at[s], sems_in.at[s]).wait()
        m = me ^ s
        live = counts[member_block(zl, zh, x, m)]
        start = first[m]
        for h in range(HQ // KVH):
            rows_q[h * BLK : (h + 1) * BLK, :] = held[s, :, h * HD : (h + 1) * HD]
            rows_g[h * BLK : (h + 1) * BLK, :] = held[s, :, WIDE + h * HD : WIDE + (h + 1) * HD]

        def place_pair(j, k_part, v_part):
            kv[j, 0:BLK, :] = k_part
            kv[j, BLK : 2 * BLK, :] = v_part
            kv_t[j, 0:BLK, :] = k_part.T
            kv_t[j, BLK : 2 * BLK, :] = v_part.T

        place_pair(0, held[s, :, 2 * WIDE : 2 * WIDE + HD], held[s, :, 2 * WIDE + HD : SLAB])

        def place_far(j, _):
            far_in(start + j - 1).wait()
            place_pair(j, far[start + j - 1, 0:BLK, :], far[start + j - 1, BLK : 2 * BLK, :])
            return 0

        lax.fori_loop(1, live, place_far, 0)

        def scores(j, tops):
            k_part = kv[j, 0:BLK, :]
            new = []
            for c in range(WIDE // LANES):
                cols = slice(c * LANES, (c + 1) * LANES)
                part = nt(k_part, rows_q[cols, :])
                expo[j, :, cols] = part
                new.append(jnp.maximum(tops[c], fold(part, jnp.max)))
            return tuple(new)

        low = jnp.full((8, LANES), -1e30, jnp.float32)
        tops = lax.fori_loop(0, live, scores, (low,) * (WIDE // LANES))
        tops = [jnp.max(a, axis=0, keepdims=True) for a in tops]

        def exps(j, sums):
            v_part = kv[j, BLK : 2 * BLK, :]
            new = []
            for c in range(WIDE // LANES):
                cols = slice(c * LANES, (c + 1) * LANES)
                e = jnp.exp((expo[j, :, cols] - tops[c]) * INV_ROOT)
                d = nt(v_part, rows_g[cols, :])
                expo[j, :, cols] = e
                dpro[j, :, cols] = d
                total, delta = sums[c]
                new.append((total + fold(e, jnp.sum), delta + fold(e * d, jnp.sum)))
            return tuple(new)

        nil = jnp.zeros((8, LANES), jnp.float32)
        sums = lax.fori_loop(0, live, exps, ((nil, nil),) * (WIDE // LANES))
        inverse, delta = [], []
        for total, weighted in sums:
            one_over = 1.0 / jnp.sum(total, axis=0, keepdims=True)
            inverse.append(one_over)
            delta.append(jnp.sum(weighted, axis=0, keepdims=True) * one_over)
        out_t[...] = jnp.zeros_like(out_t)
        dq_t[...] = jnp.zeros_like(dq_t)

        def grads(j, _):
            k_t = kv_t[j, 0:BLK, :]
            v_t = kv_t[j, BLK : 2 * BLK, :]
            dk = jnp.zeros((BLK, HD), jnp.float32)
            dv = jnp.zeros((BLK, HD), jnp.float32)
            for c in range(WIDE // LANES):
                cols = slice(c * LANES, (c + 1) * LANES)
                p = expo[j, :, cols] * inverse[c]
                ds = (p * (dpro[j, :, cols] - delta[c]) * INV_ROOT).astype(jnp.bfloat16)
                p = p.astype(jnp.bfloat16)
                out_t[:, cols] += nn(v_t, p)
                dq_t[:, cols] += nn(k_t, ds)
                dv += nn(p, rows_g[cols, :])
                dk += nn(ds, rows_q[cols, :])
            dk = dk.astype(jnp.bfloat16)
            dv = dv.astype(jnp.bfloat16)

            @pl.when(j == 0)
            def _():
                made[s, :, 2 * WIDE : 2 * WIDE + HD] = dk
                made[s, :, 2 * WIDE + HD : SLAB] = dv

            @pl.when(j > 0)
            def _():
                far_grad[start + j - 1, 0:BLK, :] = dk
                far_grad[start + j - 1, BLK : 2 * BLK, :] = dv
                far_out(start + j - 1).start()

            return 0

        lax.fori_loop(0, live, grads, 0)
        for h in range(HQ // KVH):
            cols = slice(h * HD, (h + 1) * HD)
            made[s, :, cols] = out_t[:, cols].T.astype(jnp.bfloat16)
            made[s, :, WIDE + h * HD : WIDE + (h + 1) * HD] = dq_t[:, cols].T.astype(jnp.bfloat16)
        for i in range(MEMBERS):

            @pl.when(s == i)
            def _():
                pltpu.make_async_copy(made.at[i], outs[i], sems_out.at[i]).start()

        return 0

    lax.fori_loop(0, MEMBERS, one_block, 0)
    for i in range(MEMBERS):
        pltpu.make_async_copy(made.at[i], outs[i], sems_out.at[i]).wait()

    def finish(r, _):
        far_out(r).wait()
        return 0

    lax.fori_loop(0, used, finish, 0)


def attend(place, counts, far, slabs):
    slab = jax.ShapeDtypeStruct((BLK, SLAB), jnp.bfloat16)
    result = pl.pallas_call(
        attend_kernel,
        out_shape=(slab,) * MEMBERS
        + (jax.ShapeDtypeStruct((MOST_FAR, 2 * BLK, HD), jnp.bfloat16),),
        in_specs=[smem_spec] * 2 + [any_spec] * (MEMBERS + 1),
        out_specs=(any_spec,) * (MEMBERS + 1),
        scratch_shapes=[
            pltpu.VMEM((MEMBERS, BLK, SLAB), jnp.bfloat16),
            pltpu.VMEM((MEMBERS, BLK, SLAB), jnp.bfloat16),
            pltpu.VMEM((MOST_FAR, 2 * BLK, HD), jnp.bfloat16),
            pltpu.VMEM((MOST_FAR, 2 * BLK, HD), jnp.bfloat16),
            pltpu.VMEM((WIDE, HD), jnp.bfloat16),
            pltpu.VMEM((WIDE, HD), jnp.bfloat16),
            pltpu.VMEM((MAXK, 2 * BLK, HD), jnp.bfloat16),
            pltpu.VMEM((MAXK, 2 * BLK, HD), jnp.bfloat16),
            pltpu.VMEM((MAXK, BLK, WIDE), jnp.float32),
            pltpu.VMEM((MAXK, BLK, WIDE), jnp.float32),
            pltpu.VMEM((HD, WIDE), jnp.float32),
            pltpu.VMEM((HD, WIDE), jnp.float32),
            pltpu.SMEM((MEMBERS,), jnp.int32),
            pltpu.SemaphoreType.DMA((MEMBERS,)),
            pltpu.SemaphoreType.DMA((MEMBERS,)),
            pltpu.SemaphoreType.DMA((MOST_FAR,)),
            pltpu.SemaphoreType.DMA((MOST_FAR,)),
        ],
        compiler_params=roomy,
        name="attend",
    )(place, counts, far, *slabs)
    return result[:MEMBERS], result[MEMBERS]


def trade(array, axes):
    return lax.all_to_all(array, axes, split_axis=0, concat_axis=0, tiled=True)


def swap(slabs, early=range(MEMBERS), late=()):
    done = [slabs[0]]
    for s in range(1, MEMBERS):
        slab = slabs[s]
        if s not in early:
            slab = lax.optimization_barrier((slab, *late))[0]
        done.append(lax.ppermute(slab, POOL, [(i, i ^ s) for i in range(MEMBERS)]))
    return done


def after(array, slabs):
    return lax.optimization_barrier((array, *slabs))[0]


NEAR = (4, 1)
AWAY = tuple(s for s in range(1, MEMBERS) if s not in NEAR)


def pick(meta, branches):
    which = sum((meta[1] > room).astype(jnp.int32) for room in CLASSES[:-1])
    return lax.switch(which, branches)


def body(queries, keys, values, attended_grad, key_blocks, block_counts):
    zl, zh, x = (lax.axis_index(a) for a in PLANE)
    place = jnp.stack([lax.axis_index("k") * 4 + lax.axis_index("y"), zl, zh, x])
    place = place.astype(jnp.int32)
    q, k, v, g = (a[0] for a in (queries, keys, values, attended_grad))
    src, dst, meta = make_plan(key_blocks.reshape(-1), block_counts)

    both = jnp.concatenate([k, v], axis=0)
    spread = both.reshape(4, 2, 4, 8, 2, 4, HD).transpose(0, 5, 1, 2, 4, 3, 6)
    pieces = trade(spread.reshape(NB, 8, HD), EVERY)
    slabs = swap(pack(place, q, g, k, v), NEAR, (meta,))
    pieces = after(pieces, [slabs[s] for s in NEAR])

    def bring(room):
        def run():
            sent = gather_pieces(room, src, dst, meta, pieces)
            came = trade(sent.reshape(POOLS, room, 8, HD), PLANE)
            far = came.transpose(1, 0, 2, 3).reshape(room, 2 * BLK, HD)
            return jnp.pad(far, ((0, MOST_FAR - room), (0, 0), (0, 0)))

        return run

    far = pick(meta, [bring(room) for room in CLASSES])
    made, far_grad = attend(place, block_counts, far, slabs)

    def give(room):
        def run():
            terms = far_grad[:room].reshape(room, POOLS, 8, HD).transpose(1, 0, 2, 3)
            came = trade(terms, PLANE)
            return add_pieces(room, src, dst, meta, came.reshape(POOLS * room, 8, HD))

        return run

    sums = pick(meta, [give(room) for room in CLASSES])
    traded = swap(made)
    sums = after(sums, [traded[s] for s in AWAY])
    home = trade(sums, EVERY).reshape(4, 4, 2, 4, 2, 8, HD).transpose(0, 2, 3, 5, 4, 1, 6)
    home = home.reshape(2, BLK, KVH * HD).astype(jnp.float32)
    attended, query_grad, dk, dv = unpack(place, traded)
    key_grad = (dk.astype(jnp.float32) + home[0]).astype(jnp.bfloat16)
    value_grad = (dv.astype(jnp.float32) + home[1]).astype(jnp.bfloat16)
    return attended[None], query_grad[None], key_grad[None], value_grad[None]


def solution(mesh):
    fine = Mesh(mesh.devices.reshape(SIZES), AXES)
    rows = P(*ROWS)
    return jax.shard_map(
        body,
        mesh=fine,
        in_specs=(rows,) * 4 + (P(), P()),
        out_specs=(rows,) * 4,
        check_vma=False,
    )
```

```python
import functools

import jax
import jax.numpy as jnp
from jax import lax
from jax.experimental import pallas as pl
from jax.experimental.pallas import tpu as pltpu
from jax.sharding import Mesh, PartitionSpec as P

HQ = 64
KVH = 8
HD = 128
BLK = 128
MAXK = 8
NB = 256

AXES = ("zh", "x", "k", "zl", "y")
SIZES = (2, 4, 2, 4, 4)
ROWS = (("zl", "y"), ("zh", "x", "k"), None)
POOL = ("k", "y")
PLANE = ("zl", "zh", "x")
EVERY = ("zl", "y", "zh", "x", "k")

MEMBERS = 8
POOLS = 32
MOST_FAR = MEMBERS * (MAXK - 1)
PAIR_ROOM = POOLS * MOST_FAR
STRIDE = 64
CLASSES = (24, 28, 32, 36, MOST_FAR)
UNROLL = 8
WIDE = (HQ // KVH) * HD
SLAB = 2 * WIDE + 2 * HD
LANES = 256
INV_ROOT = HD**-0.5

any_spec = pl.BlockSpec(memory_space=pl.ANY)
smem_spec = pl.BlockSpec(memory_space=pltpu.SMEM)
vmem_spec = pl.BlockSpec(memory_space=pltpu.VMEM)
roomy = pltpu.CompilerParams(vmem_limit_bytes=52 * 1024 * 1024)


def member_block(zl, zh, x, member):
    k, y = member // 4, member % 4
    return (zl * 4 + y) * 16 + zh * 8 + x * 2 + k


def plan_kernel(blocks, counts, src, dst, meta):
    def one_pool(d, carry):
        t, most = carry
        zl, zh, x = d // 8, (d // 4) % 2, d % 4

        def one_member(m, inner):
            t, r = inner
            b = member_block(zl, zh, x, m)
            extra = counts[b] - 1

            for j in range(MAXK - 1):
                src[t + j] = blocks[b * MAXK + 1 + j]
                dst[t + j] = d * STRIDE + r + j
            return (t + extra, r + extra)

        inner = (t, jnp.int32(0))
        for m in range(MEMBERS):
            inner = one_member(m, inner)
        t, r = inner
        return (t, jnp.maximum(most, r))

    total, most = lax.fori_loop(0, POOLS, one_pool, (jnp.int32(0), jnp.int32(0)))
    meta[0] = total
    meta[1] = most


def make_plan(blocks, counts):
    shape = jax.ShapeDtypeStruct((PAIR_ROOM + MAXK,), jnp.int32)
    return pl.pallas_call(
        plan_kernel,
        out_shape=(shape, shape, jax.ShapeDtypeStruct((2,), jnp.int32)),
        in_specs=[smem_spec] * 2,
        out_specs=(smem_spec,) * 3,
        name="plan",
    )(blocks, counts)


def pack_kernel(place, q, g, k, v, *rest):
    slabs, sems = rest[:MEMBERS], rest[MEMBERS]
    me = place[0]
    copies = []
    for s in range(MEMBERS):
        to = me ^ s
        wide = pl.ds(pl.multiple_of(to * WIDE, WIDE), WIDE)
        slim = pl.ds(pl.multiple_of(to * HD, HD), HD)
        parts = (
            (q.at[:, wide], slabs[s].at[:, 0:WIDE]),
            (g.at[:, wide], slabs[s].at[:, WIDE : 2 * WIDE]),
            (k.at[:, slim], slabs[s].at[:, 2 * WIDE : 2 * WIDE + HD]),
            (v.at[:, slim], slabs[s].at[:, 2 * WIDE + HD : SLAB]),
        )
        for i, (a, b) in enumerate(parts):
            copies.append(pltpu.make_async_copy(a, b, sems.at[s * 4 + i]))
    for copy in copies:
        copy.start()
    for copy in copies:
        copy.wait()


def pack(place, q, g, k, v):
    shape = jax.ShapeDtypeStruct((BLK, SLAB), jnp.bfloat16)
    return pl.pallas_call(
        pack_kernel,
        out_shape=(shape,) * MEMBERS,
        in_specs=[smem_spec] + [any_spec] * 4,
        out_specs=(vmem_spec,) * MEMBERS,
        scratch_shapes=[pltpu.SemaphoreType.DMA((4 * MEMBERS,))],
        compiler_params=roomy,
        name="pack",
    )(place, q, g, k, v)


def unpack_kernel(place, *rest):
    slabs = rest[:MEMBERS]
    out, dq, dk, dv, sems = rest[MEMBERS:]
    me = place[0]
    copies = []
    for s in range(MEMBERS):
        to = me ^ s
        wide = pl.ds(pl.multiple_of(to * WIDE, WIDE), WIDE)
        slim = pl.ds(pl.multiple_of(to * HD, HD), HD)
        parts = (
            (slabs[s].at[:, 0:WIDE], out.at[:, wide]),
            (slabs[s].at[:, WIDE : 2 * WIDE], dq.at[:, wide]),
            (slabs[s].at[:, 2 * WIDE : 2 * WIDE + HD], dk.at[:, slim]),
            (slabs[s].at[:, 2 * WIDE + HD : SLAB], dv.at[:, slim]),
        )
        for i, (a, b) in enumerate(parts):
            copies.append(pltpu.make_async_copy(a, b, sems.at[s * 4 + i]))
    for copy in copies:
        copy.start()
    for copy in copies:
        copy.wait()


def unpack(place, slabs):
    wide = jax.ShapeDtypeStruct((BLK, HQ * HD), jnp.bfloat16)
    slim = jax.ShapeDtypeStruct((BLK, KVH * HD), jnp.bfloat16)
    return pl.pallas_call(
        unpack_kernel,
        out_shape=(wide, wide, slim, slim),
        in_specs=[smem_spec] + [vmem_spec] * MEMBERS,
        out_specs=(any_spec,) * 4,
        scratch_shapes=[pltpu.SemaphoreType.DMA((4 * MEMBERS,))],
        compiler_params=roomy,
        name="unpack",
    )(place, *slabs)


def each_pair(count, one):
    def several(i, _):
        for u in range(UNROLL):
            one(i * UNROLL + u)
        return 0

    def single(t, _):
        one(t)
        return 0

    lax.fori_loop(0, count // UNROLL, several, 0)
    lax.fori_loop((count // UNROLL) * UNROLL, count, single, 0)


def gather_kernel(room, src, dst, meta, pieces, out):
    def one(t):
        at = dst[t]
        out[(at // STRIDE) * room + at % STRIDE] = pieces[src[t]]

    each_pair(meta[0], one)


def gather_pieces(room, src, dst, meta, pieces):
    return pl.pallas_call(
        functools.partial(gather_kernel, room),
        out_shape=jax.ShapeDtypeStruct((POOLS * room, 8, HD), jnp.bfloat16),
        in_specs=[smem_spec] * 3 + [vmem_spec],
        out_specs=vmem_spec,
        compiler_params=roomy,
        name="gather_pieces",
    )(src, dst, meta, pieces)


def add_kernel(room, src, dst, meta, terms, out, total):
    total[...] = jnp.zeros_like(total)

    def one(t):
        at = dst[t]
        to = src[t]
        total[to] += terms[(at // STRIDE) * room + at % STRIDE].astype(jnp.float32)

    each_pair(meta[0], one)
    out[...] = total[...].astype(jnp.bfloat16)


def add_pieces(room, src, dst, meta, terms):
    return pl.pallas_call(
        functools.partial(add_kernel, room),
        out_shape=jax.ShapeDtypeStruct((NB, 8, HD), jnp.bfloat16),
        in_specs=[smem_spec] * 3 + [vmem_spec],
        out_specs=vmem_spec,
        scratch_shapes=[pltpu.VMEM((NB, 8, HD), jnp.float32)],
        compiler_params=roomy,
        name="add_pieces",
    )(src, dst, meta, terms)


def nt(a, b):
    return lax.dot_general(a, b, (((1,), (1,)), ((), ())), preferred_element_type=jnp.float32)


def nn(a, b):
    return jnp.dot(a, b, preferred_element_type=jnp.float32)


def fold(a, how):
    return how(a.reshape(BLK // 8, 8, a.shape[1]), axis=0)


def prepare_block(held, s, rows_q, rows_g):
    for h in range(HQ // KVH):
        rows_q[h * BLK : (h + 1) * BLK, :] = held[s, :, h * HD : (h + 1) * HD]
        rows_g[h * BLK : (h + 1) * BLK, :] = held[s, :, WIDE + h * HD : WIDE + (h + 1) * HD]


def attend_kernel(place, counts, far_away, *rest):
    slabs = rest[:MEMBERS]
    own_grad, own, far_made, weights_away = rest[MEMBERS : MEMBERS + 4]
    held, far, far_grad, rows_q, rows_g, kv, expo, dpro, weights = rest[MEMBERS + 4 : MEMBERS + 13]
    first, sems_in, sems_far, sems_made, sems_weights = rest[MEMBERS + 13 :]
    me, zl, zh, x = place[0], place[1], place[2], place[3]
    for s in range(MEMBERS):
        pltpu.make_async_copy(slabs[s], held.at[s], sems_in.at[s]).start()
    base = jnp.int32(0)
    for m in range(MEMBERS):
        first[m] = base
        base = base + counts[member_block(zl, zh, x, m)] - 1
    used = base

    def far_in(r):
        return pltpu.make_async_copy(far_away.at[r], far.at[r], sems_far.at[r])

    def far_out(r):
        return pltpu.make_async_copy(far_grad.at[r], far_made.at[r], sems_made.at[r])

    def weights_out(s, j):
        slot = (s % 2) * MAXK + j
        return pltpu.make_async_copy(
            weights.at[slot], weights_away.at[s * MAXK + j], sems_weights.at[slot]
        )

    def live_in(s):
        return counts[member_block(zl, zh, x, me ^ s)]

    def weights_wait(s):
        def one(j, _):
            weights_out(s, j).wait()
            return 0

        lax.fori_loop(0, live_in(s), one, 0)

    def fetch(r, _):
        far_in(r).start()
        return 0

    lax.fori_loop(0, used, fetch, 0)

    def one_block(s, _):
        pltpu.make_async_copy(slabs[0], held.at[s], sems_in.at[s]).wait()
        live = live_in(s)
        start = first[me ^ s]
        prepare_block(held, s, rows_q, rows_g)
        kv[0, 0:BLK, :] = held[s, :, 2 * WIDE : 2 * WIDE + HD]
        kv[0, BLK : 2 * BLK, :] = held[s, :, 2 * WIDE + HD : SLAB]
        own[s] = kv[0]

        def place_far(j, _):
            far_in(start + j - 1).wait()
            kv[j] = far[start + j - 1]
            return 0

        lax.fori_loop(1, live, place_far, 0)

        def scores(j, tops):
            k_part = kv[j, 0:BLK, :]
            new = []
            for c in range(WIDE // LANES):
                cols = slice(c * LANES, (c + 1) * LANES)
                part = nt(k_part, rows_q[cols, :])
                expo[j, :, cols] = part
                new.append(jnp.maximum(tops[c], fold(part, jnp.max)))
            return tuple(new)

        low = jnp.full((8, LANES), -1e30, jnp.float32)
        tops = lax.fori_loop(0, live, scores, (low,) * (WIDE // LANES))
        tops = [jnp.max(a, axis=0, keepdims=True) for a in tops]

        def exps(j, sums):
            v_part = kv[j, BLK : 2 * BLK, :]
            new = []
            for c in range(WIDE // LANES):
                cols = slice(c * LANES, (c + 1) * LANES)
                e = jnp.exp((expo[j, :, cols] - tops[c]) * INV_ROOT)
                d = nt(v_part, rows_g[cols, :])
                expo[j, :, cols] = e
                dpro[j, :, cols] = d
                total, delta = sums[c]
                new.append((total + fold(e, jnp.sum), delta + fold(e * d, jnp.sum)))
            return tuple(new)

        nil = jnp.zeros((8, LANES), jnp.float32)
        sums = lax.fori_loop(0, live, exps, ((nil, nil),) * (WIDE // LANES))
        inverse, delta = [], []
        for total, weighted in sums:
            one_over = 1.0 / jnp.sum(total, axis=0, keepdims=True)
            inverse.append(one_over)
            delta.append(jnp.sum(weighted, axis=0, keepdims=True) * one_over)

        @pl.when(s >= 2)
        def _():
            weights_wait(s - 2)

        def grads(j, _):
            slot = (s % 2) * MAXK + j
            dk = jnp.zeros((BLK, HD), jnp.float32)
            dv = jnp.zeros((BLK, HD), jnp.float32)
            for c in range(WIDE // LANES):
                cols = slice(c * LANES, (c + 1) * LANES)
                p = expo[j, :, cols] * inverse[c]
                ds = (p * (dpro[j, :, cols] - delta[c]) * INV_ROOT).astype(jnp.bfloat16)
                p = p.astype(jnp.bfloat16)
                weights[slot, 0:BLK, cols] = p
                weights[slot, BLK : 2 * BLK, cols] = ds
                dv += nn(p, rows_g[cols, :])
                dk += nn(ds, rows_q[cols, :])
            dk = dk.astype(jnp.bfloat16)
            dv = dv.astype(jnp.bfloat16)
            weights_out(s, j).start()

            @pl.when(j == 0)
            def _():
                own_grad[s, 0:BLK, :] = dk
                own_grad[s, BLK : 2 * BLK, :] = dv

            @pl.when(j > 0)
            def _():
                far_grad[start + j - 1, 0:BLK, :] = dk
                far_grad[start + j - 1, BLK : 2 * BLK, :] = dv
                far_out(start + j - 1).start()

            return 0

        lax.fori_loop(0, live, grads, 0)
        return 0

    lax.fori_loop(0, MEMBERS, one_block, 0)
    weights_wait(MEMBERS - 2)
    weights_wait(MEMBERS - 1)

    def finish(r, _):
        far_out(r).wait()
        return 0

    lax.fori_loop(0, used, finish, 0)


def attend(place, counts, far, slabs):
    pairs = MEMBERS * MAXK
    return pl.pallas_call(
        attend_kernel,
        out_shape=(
            jax.ShapeDtypeStruct((MEMBERS, 2 * BLK, HD), jnp.bfloat16),
            jax.ShapeDtypeStruct((MEMBERS, 2 * BLK, HD), jnp.bfloat16),
            jax.ShapeDtypeStruct((MOST_FAR, 2 * BLK, HD), jnp.bfloat16),
            jax.ShapeDtypeStruct((pairs, 2 * BLK, WIDE), jnp.bfloat16),
        ),
        in_specs=[smem_spec] * 2 + [any_spec] * (MEMBERS + 1),
        out_specs=(vmem_spec, vmem_spec, any_spec, any_spec),
        scratch_shapes=[
            pltpu.VMEM((MEMBERS, BLK, SLAB), jnp.bfloat16),
            pltpu.VMEM((MOST_FAR, 2 * BLK, HD), jnp.bfloat16),
            pltpu.VMEM((MOST_FAR, 2 * BLK, HD), jnp.bfloat16),
            pltpu.VMEM((WIDE, HD), jnp.bfloat16),
            pltpu.VMEM((WIDE, HD), jnp.bfloat16),
            pltpu.VMEM((MAXK, 2 * BLK, HD), jnp.bfloat16),
            pltpu.VMEM((MAXK, BLK, WIDE), jnp.float32),
            pltpu.VMEM((MAXK, BLK, WIDE), jnp.float32),
            pltpu.VMEM((2 * MAXK, 2 * BLK, WIDE), jnp.bfloat16),
            pltpu.SMEM((MEMBERS,), jnp.int32),
            pltpu.SemaphoreType.DMA((MEMBERS,)),
            pltpu.SemaphoreType.DMA((MOST_FAR,)),
            pltpu.SemaphoreType.DMA((MOST_FAR,)),
            pltpu.SemaphoreType.DMA((2 * MAXK,)),
        ],
        compiler_params=roomy,
        name="attend",
    )(place, counts, far, *slabs)


def combine_kernel(place, counts, far_away, own_away, own_grad, weights_away, *rest):
    outs = rest[:MEMBERS]
    own, far, weights, made, out_t, dq_t = rest[MEMBERS : MEMBERS + 6]
    first, sem_own, sems_far, sems_weights, sems_out = rest[MEMBERS + 6 :]
    me, zl, zh, x = place[0], place[1], place[2], place[3]
    pltpu.make_async_copy(own_away, own, sem_own).start()
    base = jnp.int32(0)
    for m in range(MEMBERS):
        first[m] = base
        base = base + counts[member_block(zl, zh, x, m)] - 1

    def far_in(r):
        return pltpu.make_async_copy(far_away.at[r], far.at[r], sems_far.at[r])

    def weights_in(s, j):
        slot = (s % 2) * MAXK + j
        return pltpu.make_async_copy(
            weights_away.at[s * MAXK + j], weights.at[slot], sems_weights.at[slot]
        )

    def live_in(s):
        return counts[member_block(zl, zh, x, me ^ s)]

    def weights_start(s):
        def one(j, _):
            weights_in(s, j).start()
            return 0

        lax.fori_loop(0, live_in(s), one, 0)

    weights_start(0)

    def fetch(r, _):
        far_in(r).start()
        return 0

    lax.fori_loop(0, base, fetch, 0)
    pltpu.make_async_copy(own_away, own, sem_own).wait()

    def one_block(s, _):
        @pl.when(s + 1 < MEMBERS)
        def _():
            weights_start(s + 1)

        live = live_in(s)
        start = first[me ^ s]

        def add_pair(j, k_part, v_part, fresh):
            slot = (s % 2) * MAXK + j
            weights_in(s, j).wait()
            k_t, v_t = k_part.T, v_part.T
            for c in range(WIDE // LANES):
                cols = slice(c * LANES, (c + 1) * LANES)
                o = nn(v_t, weights[slot, 0:BLK, cols])
                d = nn(k_t, weights[slot, BLK : 2 * BLK, cols])
                if fresh:
                    out_t[:, cols] = o
                    dq_t[:, cols] = d
                else:
                    out_t[:, cols] += o
                    dq_t[:, cols] += d

        add_pair(0, own[s, 0:BLK, :], own[s, BLK : 2 * BLK, :], True)

        def add_far(j, _):
            r = start + j - 1
            far_in(r).wait()
            add_pair(j, far[r, 0:BLK, :], far[r, BLK : 2 * BLK, :], False)
            return 0

        lax.fori_loop(1, live, add_far, 0)
        for h in range(HQ // KVH):
            cols = slice(h * HD, (h + 1) * HD)
            made[s, :, cols] = out_t[:, cols].T.astype(jnp.bfloat16)
            made[s, :, WIDE + h * HD : WIDE + (h + 1) * HD] = dq_t[:, cols].T.astype(jnp.bfloat16)
        made[s, :, 2 * WIDE : 2 * WIDE + HD] = own_grad[s, 0:BLK, :]
        made[s, :, 2 * WIDE + HD : SLAB] = own_grad[s, BLK : 2 * BLK, :]
        for i in range(MEMBERS):

            @pl.when(s == i)
            def _():
                pltpu.make_async_copy(made.at[i], outs[i], sems_out.at[i]).start()

        return 0

    lax.fori_loop(0, MEMBERS, one_block, 0)
    for i in range(MEMBERS):
        pltpu.make_async_copy(made.at[i], outs[i], sems_out.at[i]).wait()


def combine(place, counts, far, own, own_grad, weights):
    slab = jax.ShapeDtypeStruct((BLK, SLAB), jnp.bfloat16)
    return pl.pallas_call(
        combine_kernel,
        out_shape=(slab,) * MEMBERS,
        in_specs=[smem_spec] * 2 + [any_spec] * 2 + [vmem_spec] + [any_spec],
        out_specs=(any_spec,) * MEMBERS,
        scratch_shapes=[
            pltpu.VMEM((MEMBERS, 2 * BLK, HD), jnp.bfloat16),
            pltpu.VMEM((MOST_FAR, 2 * BLK, HD), jnp.bfloat16),
            pltpu.VMEM((2 * MAXK, 2 * BLK, WIDE), jnp.bfloat16),
            pltpu.VMEM((MEMBERS, BLK, SLAB), jnp.bfloat16),
            pltpu.VMEM((HD, WIDE), jnp.float32),
            pltpu.VMEM((HD, WIDE), jnp.float32),
            pltpu.SMEM((MEMBERS,), jnp.int32),
            pltpu.SemaphoreType.DMA,
            pltpu.SemaphoreType.DMA((MOST_FAR,)),
            pltpu.SemaphoreType.DMA((2 * MAXK,)),
            pltpu.SemaphoreType.DMA((MEMBERS,)),
        ],
        compiler_params=roomy,
        cost_estimate=pl.CostEstimate(
            flops=32 * 4 * BLK * BLK * WIDE, bytes_accessed=32 * 1024 * 1024, transcendentals=0
        ),
        name="combine",
    )(place, counts, far, own, own_grad, weights)


def trade(array, axes):
    return lax.all_to_all(array, axes, split_axis=0, concat_axis=0, tiled=True)


def swap(slabs, early=range(MEMBERS), late=()):
    done = [slabs[0]]
    for s in range(1, MEMBERS):
        slab = slabs[s]
        if s not in early:
            slab = lax.optimization_barrier((slab, *late))[0]
        done.append(lax.ppermute(slab, POOL, [(i, i ^ s) for i in range(MEMBERS)]))
    return done


def after(array, slabs):
    return lax.optimization_barrier((array, *slabs))[0]


NEAR = (4, 1)
ONE_HOP = (4, 1, 3, 5, 7)
AWAY = tuple(s for s in range(1, MEMBERS) if s not in NEAR)


def pick(meta, branches):
    which = sum((meta[1] > room).astype(jnp.int32) for room in CLASSES[:-1])
    return lax.switch(which, branches)


def body(queries, keys, values, attended_grad, key_blocks, block_counts):
    zl, zh, x = (lax.axis_index(a) for a in PLANE)
    place = jnp.stack([lax.axis_index("k") * 4 + lax.axis_index("y"), zl, zh, x])
    place = place.astype(jnp.int32)
    q, k, v, g = (a[0] for a in (queries, keys, values, attended_grad))
    src, dst, meta = make_plan(key_blocks.reshape(-1), block_counts)

    both = jnp.concatenate([k, v], axis=0)
    spread = both.reshape(4, 2, 4, 8, 2, 4, HD).transpose(0, 5, 1, 2, 4, 3, 6)
    pieces = trade(spread.reshape(NB, 8, HD), EVERY)
    slabs = swap(pack(place, q, g, k, v), NEAR, (meta,))
    pieces = after(pieces, [slabs[s] for s in NEAR])

    def bring(room):
        def run():
            sent = gather_pieces(room, src, dst, meta, pieces)
            came = trade(sent.reshape(POOLS, room, 8, HD), PLANE)
            far = came.transpose(1, 0, 2, 3).reshape(room, 2 * BLK, HD)
            return jnp.pad(far, ((0, MOST_FAR - room), (0, 0), (0, 0)))

        return run

    far = pick(meta, [bring(room) for room in CLASSES])
    own_grad, own, far_grad, weights = attend(place, block_counts, far, slabs)

    def give(room):
        def run():
            terms = far_grad[:room].reshape(room, POOLS, 8, HD).transpose(1, 0, 2, 3)
            came = trade(terms, PLANE)
            made = combine(place, block_counts, far, own, own_grad, weights)
            traded = swap(made)
            sums = add_pieces(room, src, dst, meta, came.reshape(POOLS * room, 8, HD))
            sums = after(sums, [traded[s] for s in ONE_HOP])
            home = trade(sums, EVERY).reshape(4, 4, 2, 4, 2, 8, HD).transpose(0, 2, 3, 5, 4, 1, 6)
            home = home.reshape(2, BLK, KVH * HD).astype(jnp.float32)
            attended, query_grad, dk, dv = unpack(place, traded)
            key_grad = (dk.astype(jnp.float32) + home[0]).astype(jnp.bfloat16)
            value_grad = (dv.astype(jnp.float32) + home[1]).astype(jnp.bfloat16)
            return attended[None], query_grad[None], key_grad[None], value_grad[None]

        return run

    return pick(meta, [give(room) for room in CLASSES])


def solution(mesh):
    fine = Mesh(mesh.devices.reshape(SIZES), AXES)
    rows = P(*ROWS)
    return jax.shard_map(
        body,
        mesh=fine,
        in_specs=(rows,) * 4 + (P(), P()),
        out_specs=(rows,) * 4,
        check_vma=False,
    )
```

```python
import functools

import jax
import jax.numpy as jnp
from jax import lax
from jax.experimental import pallas as pl
from jax.experimental.pallas import tpu as pltpu
from jax.sharding import Mesh, PartitionSpec as P

HQ = 64
KVH = 8
HD = 128
BLK = 128
MAXK = 8
NB = 256

AXES = ("zh", "x", "k", "zl", "y")
SIZES = (2, 4, 2, 4, 4)
ROWS = (("zl", "y"), ("zh", "x", "k"), None)
POOL = ("k", "y")
PLANE = ("zl", "zh", "x")
EVERY = ("zl", "y", "zh", "x", "k")

MEMBERS = 8
POOLS = 32
MOST_FAR = MEMBERS * (MAXK - 1)
PAIR_ROOM = POOLS * MOST_FAR
STRIDE = 64
CLASSES = (28, 34, MOST_FAR)
UNROLL = 8
WIDE = (HQ // KVH) * HD
SLAB = 2 * WIDE + 2 * HD
LANES = 256
INV_ROOT = HD**-0.5

any_spec = pl.BlockSpec(memory_space=pl.ANY)
smem_spec = pl.BlockSpec(memory_space=pltpu.SMEM)
vmem_spec = pl.BlockSpec(memory_space=pltpu.VMEM)
roomy = pltpu.CompilerParams(vmem_limit_bytes=52 * 1024 * 1024)


def member_block(zl, zh, x, member):
    k, y = member // 4, member % 4
    return (zl * 4 + y) * 16 + zh * 8 + x * 2 + k


def plan_kernel(blocks, counts, src, dst, meta):
    def one_pool(d, carry):
        t, most = carry
        zl, zh, x = d // 8, (d // 4) % 2, d % 4

        def one_member(m, inner):
            t, r = inner
            b = member_block(zl, zh, x, m)
            extra = counts[b] - 1

            for j in range(MAXK - 1):
                src[t + j] = blocks[b * MAXK + 1 + j]
                dst[t + j] = d * STRIDE + r + j
            return (t + extra, r + extra)

        inner = (t, jnp.int32(0))
        for m in range(MEMBERS):
            inner = one_member(m, inner)
        t, r = inner
        return (t, jnp.maximum(most, r))

    total, most = lax.fori_loop(0, POOLS, one_pool, (jnp.int32(0), jnp.int32(0)))
    meta[0] = total
    meta[1] = most


def make_plan(blocks, counts):
    shape = jax.ShapeDtypeStruct((PAIR_ROOM + MAXK,), jnp.int32)
    return pl.pallas_call(
        plan_kernel,
        out_shape=(shape, shape, jax.ShapeDtypeStruct((2,), jnp.int32)),
        in_specs=[smem_spec] * 2,
        out_specs=(smem_spec,) * 3,
        name="plan",
    )(blocks, counts)


def pack_kernel(place, q, g, k, v, *rest):
    slabs, sems = rest[:MEMBERS], rest[MEMBERS]
    me = place[0]
    copies = []
    for s in range(MEMBERS):
        to = me ^ s
        wide = pl.ds(pl.multiple_of(to * WIDE, WIDE), WIDE)
        slim = pl.ds(pl.multiple_of(to * HD, HD), HD)
        parts = (
            (q.at[:, wide], slabs[s].at[:, 0:WIDE]),
            (g.at[:, wide], slabs[s].at[:, WIDE : 2 * WIDE]),
            (k.at[:, slim], slabs[s].at[:, 2 * WIDE : 2 * WIDE + HD]),
            (v.at[:, slim], slabs[s].at[:, 2 * WIDE + HD : SLAB]),
        )
        for i, (a, b) in enumerate(parts):
            copies.append(pltpu.make_async_copy(a, b, sems.at[s * 4 + i]))
    for copy in copies:
        copy.start()
    for copy in copies:
        copy.wait()


def pack(place, q, g, k, v):
    shape = jax.ShapeDtypeStruct((BLK, SLAB), jnp.bfloat16)
    return pl.pallas_call(
        pack_kernel,
        out_shape=(shape,) * MEMBERS,
        in_specs=[smem_spec] + [any_spec] * 4,
        out_specs=(vmem_spec,) * MEMBERS,
        scratch_shapes=[pltpu.SemaphoreType.DMA((4 * MEMBERS,))],
        compiler_params=roomy,
        name="pack",
    )(place, q, g, k, v)


def unpack_kernel(place, *rest):
    slabs = rest[:MEMBERS]
    out, dq, dk, dv, sems = rest[MEMBERS:]
    me = place[0]
    copies = []
    for s in range(MEMBERS):
        to = me ^ s
        wide = pl.ds(pl.multiple_of(to * WIDE, WIDE), WIDE)
        slim = pl.ds(pl.multiple_of(to * HD, HD), HD)
        parts = (
            (slabs[s].at[:, 0:WIDE], out.at[:, wide]),
            (slabs[s].at[:, WIDE : 2 * WIDE], dq.at[:, wide]),
            (slabs[s].at[:, 2 * WIDE : 2 * WIDE + HD], dk.at[:, slim]),
            (slabs[s].at[:, 2 * WIDE + HD : SLAB], dv.at[:, slim]),
        )
        for i, (a, b) in enumerate(parts):
            copies.append(pltpu.make_async_copy(a, b, sems.at[s * 4 + i]))
    for copy in copies:
        copy.start()
    for copy in copies:
        copy.wait()


def unpack(place, slabs):
    wide = jax.ShapeDtypeStruct((BLK, HQ * HD), jnp.bfloat16)
    slim = jax.ShapeDtypeStruct((BLK, KVH * HD), jnp.bfloat16)
    return pl.pallas_call(
        unpack_kernel,
        out_shape=(wide, wide, slim, slim),
        in_specs=[smem_spec] + [vmem_spec] * MEMBERS,
        out_specs=(any_spec,) * 4,
        scratch_shapes=[pltpu.SemaphoreType.DMA((4 * MEMBERS,))],
        compiler_params=roomy,
        name="unpack",
    )(place, *slabs)


def each_pair(count, one):
    def several(i, _):
        for u in range(UNROLL):
            one(i * UNROLL + u)
        return 0

    def single(t, _):
        one(t)
        return 0

    lax.fori_loop(0, count // UNROLL, several, 0)
    lax.fori_loop((count // UNROLL) * UNROLL, count, single, 0)


def gather_kernel(room, src, dst, meta, pieces, out):
    def one(t):
        at = dst[t]
        out[(at // STRIDE) * room + at % STRIDE] = pieces[src[t]]

    each_pair(meta[0], one)


def gather_pieces(room, src, dst, meta, pieces):
    return pl.pallas_call(
        functools.partial(gather_kernel, room),
        out_shape=jax.ShapeDtypeStruct((POOLS * room, 8, HD), jnp.bfloat16),
        in_specs=[smem_spec] * 3 + [vmem_spec],
        out_specs=vmem_spec,
        compiler_params=roomy,
        name="gather_pieces",
    )(src, dst, meta, pieces)


def add_kernel(room, src, dst, meta, terms, out, total):
    total[...] = jnp.zeros_like(total)

    def one(t):
        at = dst[t]
        to = src[t]
        total[to] += terms[(at // STRIDE) * room + at % STRIDE].astype(jnp.float32)

    each_pair(meta[0], one)
    out[...] = total[...].astype(jnp.bfloat16)


def add_pieces(room, src, dst, meta, terms):
    return pl.pallas_call(
        functools.partial(add_kernel, room),
        out_shape=jax.ShapeDtypeStruct((NB, 8, HD), jnp.bfloat16),
        in_specs=[smem_spec] * 3 + [vmem_spec],
        out_specs=vmem_spec,
        scratch_shapes=[pltpu.VMEM((NB, 8, HD), jnp.float32)],
        compiler_params=roomy,
        name="add_pieces",
    )(src, dst, meta, terms)


def nt(a, b):
    return lax.dot_general(a, b, (((1,), (1,)), ((), ())), preferred_element_type=jnp.float32)


def nn(a, b):
    return jnp.dot(a, b, preferred_element_type=jnp.float32)


def fold(a, how):
    return how(a.reshape(BLK // 8, 8, a.shape[1]), axis=0)


def prepare_block(held, s, rows_q, rows_g):
    for h in range(HQ // KVH):
        rows_q[h * BLK : (h + 1) * BLK, :] = held[s, :, h * HD : (h + 1) * HD]
        rows_g[h * BLK : (h + 1) * BLK, :] = held[s, :, WIDE + h * HD : WIDE + (h + 1) * HD]


def attend_kernel(place, counts, far_away, *rest):
    slabs = rest[:MEMBERS]
    own_grad, own, far_made, weights_away = rest[MEMBERS : MEMBERS + 4]
    held, far, far_grad, rows_q, rows_g, kv, expo, dpro, weights = rest[MEMBERS + 4 : MEMBERS + 13]
    first, sems_in, sems_far, sems_made, sems_weights = rest[MEMBERS + 13 :]
    me, zl, zh, x = place[0], place[1], place[2], place[3]
    for s in range(MEMBERS):
        pltpu.make_async_copy(slabs[s], held.at[s], sems_in.at[s]).start()
    base = jnp.int32(0)
    for m in range(MEMBERS):
        first[m] = base
        base = base + counts[member_block(zl, zh, x, m)] - 1
    used = base

    def far_in(r):
        return pltpu.make_async_copy(far_away.at[r], far.at[r], sems_far.at[r])

    def far_out(r):
        return pltpu.make_async_copy(far_grad.at[r], far_made.at[r], sems_made.at[r])

    def weights_out(s, j):
        slot = (s % 2) * MAXK + j
        return pltpu.make_async_copy(
            weights.at[slot], weights_away.at[s * MAXK + j], sems_weights.at[slot]
        )

    def live_in(s):
        return counts[member_block(zl, zh, x, me ^ s)]

    def weights_wait(s):
        def one(j, _):
            weights_out(s, j).wait()
            return 0

        lax.fori_loop(0, live_in(s), one, 0)

    def fetch(r, _):
        far_in(r).start()
        return 0

    lax.fori_loop(0, used, fetch, 0)

    def one_block(s, _):
        pltpu.make_async_copy(slabs[0], held.at[s], sems_in.at[s]).wait()
        live = live_in(s)
        start = first[me ^ s]
        prepare_block(held, s, rows_q, rows_g)
        kv[0, 0:BLK, :] = held[s, :, 2 * WIDE : 2 * WIDE + HD]
        kv[0, BLK : 2 * BLK, :] = held[s, :, 2 * WIDE + HD : SLAB]
        own[s] = kv[0]

        def place_far(j, _):
            far_in(start + j - 1).wait()
            kv[j] = far[start + j - 1]
            return 0

        lax.fori_loop(1, live, place_far, 0)

        def scores(j, tops):
            k_part = kv[j, 0:BLK, :]
            new = []
            for c in range(WIDE // LANES):
                cols = slice(c * LANES, (c + 1) * LANES)
                part = nt(k_part, rows_q[cols, :])
                expo[j, :, cols] = part
                new.append(jnp.maximum(tops[c], fold(part, jnp.max)))
            return tuple(new)

        low = jnp.full((8, LANES), -1e30, jnp.float32)
        tops = lax.fori_loop(0, live, scores, (low,) * (WIDE // LANES))
        tops = [jnp.max(a, axis=0, keepdims=True) for a in tops]

        def exps(j, sums):
            v_part = kv[j, BLK : 2 * BLK, :]
            new = []
            for c in range(WIDE // LANES):
                cols = slice(c * LANES, (c + 1) * LANES)
                e = jnp.exp((expo[j, :, cols] - tops[c]) * INV_ROOT)
                d = nt(v_part, rows_g[cols, :])
                expo[j, :, cols] = e
                dpro[j, :, cols] = d
                total, delta = sums[c]
                new.append((total + fold(e, jnp.sum), delta + fold(e * d, jnp.sum)))
            return tuple(new)

        nil = jnp.zeros((8, LANES), jnp.float32)
        sums = lax.fori_loop(0, live, exps, ((nil, nil),) * (WIDE // LANES))
        inverse, delta = [], []
        for total, weighted in sums:
            one_over = 1.0 / jnp.sum(total, axis=0, keepdims=True)
            inverse.append(one_over)
            delta.append(jnp.sum(weighted, axis=0, keepdims=True) * one_over)

        @pl.when(s >= 2)
        def _():
            weights_wait(s - 2)

        def grads(j, _):
            slot = (s % 2) * MAXK + j
            dk = jnp.zeros((BLK, HD), jnp.float32)
            dv = jnp.zeros((BLK, HD), jnp.float32)
            for c in range(WIDE // LANES):
                cols = slice(c * LANES, (c + 1) * LANES)
                p = expo[j, :, cols] * inverse[c]
                ds = (p * (dpro[j, :, cols] - delta[c]) * INV_ROOT).astype(jnp.bfloat16)
                p = p.astype(jnp.bfloat16)
                weights[slot, 0:BLK, cols] = p
                weights[slot, BLK : 2 * BLK, cols] = ds
                dv += nn(p, rows_g[cols, :])
                dk += nn(ds, rows_q[cols, :])
            dk = dk.astype(jnp.bfloat16)
            dv = dv.astype(jnp.bfloat16)
            weights_out(s, j).start()

            @pl.when(j == 0)
            def _():
                own_grad[s, 0:BLK, :] = dk
                own_grad[s, BLK : 2 * BLK, :] = dv

            @pl.when(j > 0)
            def _():
                far_grad[start + j - 1, 0:BLK, :] = dk
                far_grad[start + j - 1, BLK : 2 * BLK, :] = dv
                far_out(start + j - 1).start()

            return 0

        lax.fori_loop(0, live, grads, 0)
        return 0

    lax.fori_loop(0, MEMBERS, one_block, 0)
    weights_wait(MEMBERS - 2)
    weights_wait(MEMBERS - 1)

    def finish(r, _):
        far_out(r).wait()
        return 0

    lax.fori_loop(0, used, finish, 0)


def attend(place, counts, far, slabs):
    pairs = MEMBERS * MAXK
    return pl.pallas_call(
        attend_kernel,
        out_shape=(
            jax.ShapeDtypeStruct((MEMBERS, 2 * BLK, HD), jnp.bfloat16),
            jax.ShapeDtypeStruct((MEMBERS, 2 * BLK, HD), jnp.bfloat16),
            jax.ShapeDtypeStruct((MOST_FAR, 2 * BLK, HD), jnp.bfloat16),
            jax.ShapeDtypeStruct((pairs, 2 * BLK, WIDE), jnp.bfloat16),
        ),
        in_specs=[smem_spec] * 2 + [any_spec] * (MEMBERS + 1),
        out_specs=(vmem_spec, vmem_spec, any_spec, any_spec),
        scratch_shapes=[
            pltpu.VMEM((MEMBERS, BLK, SLAB), jnp.bfloat16),
            pltpu.VMEM((MOST_FAR, 2 * BLK, HD), jnp.bfloat16),
            pltpu.VMEM((MOST_FAR, 2 * BLK, HD), jnp.bfloat16),
            pltpu.VMEM((WIDE, HD), jnp.bfloat16),
            pltpu.VMEM((WIDE, HD), jnp.bfloat16),
            pltpu.VMEM((MAXK, 2 * BLK, HD), jnp.bfloat16),
            pltpu.VMEM((MAXK, BLK, WIDE), jnp.float32),
            pltpu.VMEM((MAXK, BLK, WIDE), jnp.float32),
            pltpu.VMEM((2 * MAXK, 2 * BLK, WIDE), jnp.bfloat16),
            pltpu.SMEM((MEMBERS,), jnp.int32),
            pltpu.SemaphoreType.DMA((MEMBERS,)),
            pltpu.SemaphoreType.DMA((MOST_FAR,)),
            pltpu.SemaphoreType.DMA((MOST_FAR,)),
            pltpu.SemaphoreType.DMA((2 * MAXK,)),
        ],
        compiler_params=roomy,
        name="attend",
    )(place, counts, far, *slabs)


def combine_kernel(place, counts, far_away, own_away, own_grad, weights_away, *rest):
    outs = rest[:MEMBERS]
    own, far, weights, made, out_t, dq_t = rest[MEMBERS : MEMBERS + 6]
    first, sem_own, sems_far, sems_weights, sems_out = rest[MEMBERS + 6 :]
    me, zl, zh, x = place[0], place[1], place[2], place[3]
    pltpu.make_async_copy(own_away, own, sem_own).start()
    base = jnp.int32(0)
    for m in range(MEMBERS):
        first[m] = base
        base = base + counts[member_block(zl, zh, x, m)] - 1

    def far_in(r):
        return pltpu.make_async_copy(far_away.at[r], far.at[r], sems_far.at[r])

    def weights_in(s, j):
        slot = (s % 2) * MAXK + j
        return pltpu.make_async_copy(
            weights_away.at[s * MAXK + j], weights.at[slot], sems_weights.at[slot]
        )

    def live_in(s):
        return counts[member_block(zl, zh, x, me ^ s)]

    def weights_start(s):
        def one(j, _):
            weights_in(s, j).start()
            return 0

        lax.fori_loop(0, live_in(s), one, 0)

    weights_start(0)

    def fetch(r, _):
        far_in(r).start()
        return 0

    lax.fori_loop(0, base, fetch, 0)
    pltpu.make_async_copy(own_away, own, sem_own).wait()

    def one_block(s, _):
        @pl.when(s + 1 < MEMBERS)
        def _():
            weights_start(s + 1)

        live = live_in(s)
        start = first[me ^ s]

        def add_pair(j, k_part, v_part, fresh):
            slot = (s % 2) * MAXK + j
            weights_in(s, j).wait()
            k_t, v_t = k_part.T, v_part.T
            for c in range(WIDE // LANES):
                cols = slice(c * LANES, (c + 1) * LANES)
                o = nn(v_t, weights[slot, 0:BLK, cols])
                d = nn(k_t, weights[slot, BLK : 2 * BLK, cols])
                if fresh:
                    out_t[:, cols] = o
                    dq_t[:, cols] = d
                else:
                    out_t[:, cols] += o
                    dq_t[:, cols] += d

        add_pair(0, own[s, 0:BLK, :], own[s, BLK : 2 * BLK, :], True)

        def add_far(j, _):
            r = start + j - 1
            far_in(r).wait()
            add_pair(j, far[r, 0:BLK, :], far[r, BLK : 2 * BLK, :], False)
            return 0

        lax.fori_loop(1, live, add_far, 0)
        for h in range(HQ // KVH):
            cols = slice(h * HD, (h + 1) * HD)
            made[s, :, cols] = out_t[:, cols].T.astype(jnp.bfloat16)
            made[s, :, WIDE + h * HD : WIDE + (h + 1) * HD] = dq_t[:, cols].T.astype(jnp.bfloat16)
        made[s, :, 2 * WIDE : 2 * WIDE + HD] = own_grad[s, 0:BLK, :]
        made[s, :, 2 * WIDE + HD : SLAB] = own_grad[s, BLK : 2 * BLK, :]
        for i in range(MEMBERS):

            @pl.when(s == i)
            def _():
                pltpu.make_async_copy(made.at[i], outs[i], sems_out.at[i]).start()

        return 0

    lax.fori_loop(0, MEMBERS, one_block, 0)
    for i in range(MEMBERS):
        pltpu.make_async_copy(made.at[i], outs[i], sems_out.at[i]).wait()


def combine(place, counts, far, own, own_grad, weights):
    slab = jax.ShapeDtypeStruct((BLK, SLAB), jnp.bfloat16)
    return pl.pallas_call(
        combine_kernel,
        out_shape=(slab,) * MEMBERS,
        in_specs=[smem_spec] * 2 + [any_spec] * 2 + [vmem_spec] + [any_spec],
        out_specs=(any_spec,) * MEMBERS,
        scratch_shapes=[
            pltpu.VMEM((MEMBERS, 2 * BLK, HD), jnp.bfloat16),
            pltpu.VMEM((MOST_FAR, 2 * BLK, HD), jnp.bfloat16),
            pltpu.VMEM((2 * MAXK, 2 * BLK, WIDE), jnp.bfloat16),
            pltpu.VMEM((MEMBERS, BLK, SLAB), jnp.bfloat16),
            pltpu.VMEM((HD, WIDE), jnp.float32),
            pltpu.VMEM((HD, WIDE), jnp.float32),
            pltpu.SMEM((MEMBERS,), jnp.int32),
            pltpu.SemaphoreType.DMA,
            pltpu.SemaphoreType.DMA((MOST_FAR,)),
            pltpu.SemaphoreType.DMA((2 * MAXK,)),
            pltpu.SemaphoreType.DMA((MEMBERS,)),
        ],
        compiler_params=roomy,
        cost_estimate=pl.CostEstimate(
            flops=32 * 4 * BLK * BLK * WIDE, bytes_accessed=32 * 1024 * 1024, transcendentals=0
        ),
        name="combine",
    )(place, counts, far, own, own_grad, weights)


def trade(array, axes):
    return lax.all_to_all(array, axes, split_axis=0, concat_axis=0, tiled=True)


def swap(slabs, early=range(MEMBERS), late=()):
    done = [slabs[0]]
    for s in range(1, MEMBERS):
        slab = slabs[s]
        if s not in early:
            slab = lax.optimization_barrier((slab, *late))[0]
        done.append(lax.ppermute(slab, POOL, [(i, i ^ s) for i in range(MEMBERS)]))
    return done


def after(array, slabs):
    return lax.optimization_barrier((array, *slabs))[0]


NEAR = (4, 1)
ONE_HOP = (4, 1, 3, 5, 7)
AWAY = tuple(s for s in range(1, MEMBERS) if s not in NEAR)


def pick(meta, branches):
    which = sum((meta[1] > room).astype(jnp.int32) for room in CLASSES[:-1])
    return lax.switch(which, branches)


def body(queries, keys, values, attended_grad, key_blocks, block_counts):
    zl, zh, x = (lax.axis_index(a) for a in PLANE)
    place = jnp.stack([lax.axis_index("k") * 4 + lax.axis_index("y"), zl, zh, x])
    place = place.astype(jnp.int32)
    q, k, v, g = (a[0] for a in (queries, keys, values, attended_grad))
    src, dst, meta = make_plan(key_blocks.reshape(-1), block_counts)

    both = jnp.concatenate([k, v], axis=0)
    spread = both.reshape(4, 2, 4, 8, 2, 4, HD).transpose(0, 5, 1, 2, 4, 3, 6)
    pieces = trade(spread.reshape(NB, 8, HD), EVERY)
    slabs = swap(pack(place, q, g, k, v), NEAR, (meta,))
    pieces = after(pieces, [slabs[s] for s in NEAR])

    def bring(room):
        def run():
            sent = gather_pieces(room, src, dst, meta, pieces)
            came = trade(sent.reshape(POOLS, room, 8, HD), PLANE)
            far = came.transpose(1, 0, 2, 3).reshape(room, 2 * BLK, HD)
            return jnp.pad(far, ((0, MOST_FAR - room), (0, 0), (0, 0)))

        return run

    far = pick(meta, [bring(room) for room in CLASSES])
    own_grad, own, far_grad, weights = attend(place, block_counts, far, slabs)

    def give(room):
        def run():
            terms = far_grad[:room].reshape(room, POOLS, 8, HD).transpose(1, 0, 2, 3)
            came = trade(terms, PLANE)
            made = combine(place, block_counts, far, own, own_grad, weights)
            traded = swap(made)
            sums = add_pieces(room, src, dst, meta, came.reshape(POOLS * room, 8, HD))
            sums = after(sums, [traded[s] for s in ONE_HOP])
            home = trade(sums, EVERY).reshape(4, 4, 2, 4, 2, 8, HD).transpose(0, 2, 3, 5, 4, 1, 6)
            home = home.reshape(2, BLK, KVH * HD).astype(jnp.float32)
            attended, query_grad, dk, dv = unpack(place, traded)
            key_grad = (dk.astype(jnp.float32) + home[0]).astype(jnp.bfloat16)
            value_grad = (dv.astype(jnp.float32) + home[1]).astype(jnp.bfloat16)
            return attended[None], query_grad[None], key_grad[None], value_grad[None]

        return run

    return pick(meta, [give(room) for room in CLASSES])


def solution(mesh):
    fine = Mesh(mesh.devices.reshape(SIZES), AXES)
    rows = P(*ROWS)
    return jax.shard_map(
        body,
        mesh=fine,
        in_specs=(rows,) * 4 + (P(), P()),
        out_specs=(rows,) * 4,
        check_vma=False,
    )
```
